512 devices in a mesh: gx: 32 (over x, y), gy: 16 (over z, core).
Axes of the slice: x: 4, y: 8, z: 8, core: 2. Of those that a mesh axis runs over, the one named last changes fastest.
Arguments:
- density: bfloat16 [32, 16, 8, 131072], P('gx', 'gy'), may hold values from 3.1232834e-05 to 0.050048828
- source: bfloat16 [32, 16, 8, 131072], P('gx', 'gy'), may hold values from 0.5 to 4
- occupancy: int32 [32, 16, 1024], P('gx', 'gy'), may hold values from 0 to 1, as said below
- row_order: int32 [16], replicated, may hold values from 0 to 15, each once
- col_order: int32 [32], replicated, may hold values from 0 to 31, each once
Outputs:
- emission: float32 [131072], P(('gx', 'gy'))
- transmittance: float32 [131072], P(('gx', 'gy'))
The draws below stay inside these ranges and needn't reach their ends.
Inputs may be any that keep to these rules, and one draw needn't show every extreme that they name: `occupancy`: each brick's 1 entries lie in one band of 102 consecutive blocks, counted cyclically over the 1024 blocks; the band's first and last blocks are 1.
All inputs are finite; a program needn't handle non-finite values.
Results may differ from the reference program's by a relative error of at most 0.0003.
Values sent between devices are 32-bit elements; how exact they have to be, the bound alone decides.
A program may use at most 64 MiB of HBM per device.

```python
import math
import jax
import jax.numpy as jnp
from jax import lax

DEPTH = 8
BLOCK = 128
PIX = 131072
NBLK = 1024
FOOT = 102
N_GX = 32
N_GY = 16
DEVICES = 512


def draw_occupancy(key, part):
    key = jax.random.fold_in(key, 7)
    first_key, second_key = jax.random.split(key)
    shape = (N_GX, N_GY, NBLK)
    col_ids = lax.broadcasted_iota(jnp.int32, shape, 0)
    row_ids = lax.broadcasted_iota(jnp.int32, shape, 1)
    blk_ids = lax.broadcasted_iota(jnp.int32, shape, 2)
    jitter = jax.random.randint(first_key, (N_GX, N_GY, 1), 0, max(2, FOOT))
    brick = row_ids * N_GX + col_ids
    start = (brick * NBLK // DEVICES + jitter) % NBLK
    offset = (blk_ids - start) % NBLK
    inside = offset < FOOT
    ends = (offset == 0) | (offset == FOOT - 1)
    kept = jax.random.randint(second_key, shape, 0, 5) > 0
    return (inside & (kept | ends)).astype(jnp.int32)


def steps_of(rng, dims, cuts, least, high):
    loudness, own = 1.0, jax.random.fold_in(rng, 6)
    for dim, shards_of in cuts:
        steps = jnp.exp(jax.random.uniform(jax.random.fold_in(own, dim), (shards_of,), jnp.float32, least / len(cuts), high / len(cuts)))
        loudness = loudness * jnp.repeat(steps, dims[dim] // shards_of).reshape([-1 if axis == dim else 1 for axis in range(len(dims))])
    return loudness


def setup_inputs(seed: int = 0) -> dict:
    key_of = jax.random.split(jax.random.key(seed), 6)
    return {
        "density": jnp.clip(jnp.exp(math.log(0.050048828) - 7.3792845 * jax.random.uniform(key_of[0], (N_GX, N_GY, DEPTH, PIX), jnp.float32) ** steps_of(key_of[0], (N_GX, N_GY, DEPTH, PIX), ((0, 32), (1, 16)), -0.2, 0.2)), 3.123283386230469e-05, 0.050048828).astype(jnp.bfloat16),
        "source": jnp.clip(0.5 + 3.5 * jax.random.uniform(key_of[1], (N_GX, N_GY, DEPTH, PIX), jnp.float32) ** steps_of(key_of[1], (N_GX, N_GY, DEPTH, PIX), ((0, 32), (1, 16)), -0.2, 0.2), 0.5, 4.0).astype(jnp.bfloat16),
        "occupancy": draw_occupancy(jax.random.fold_in(key_of[5], 71), 0),
        "row_order": jax.random.permutation(key_of[3], N_GY).astype(jnp.int32),
        "col_order": jax.random.permutation(key_of[4], N_GX).astype(jnp.int32),
    }


def shade_brick(density_brick, source_brick, occupancy_brick):
    occupied = occupancy_brick.astype(jnp.float32)[:, None]
    color = jnp.zeros((NBLK, BLOCK), jnp.float32)
    trans = jnp.ones((NBLK, BLOCK), jnp.float32)
    for sample in range(DEPTH):
        tau = density_brick[sample].astype(jnp.float32).reshape(NBLK, BLOCK) * occupied
        fade = jnp.exp(-tau)
        color = color + trans * source_brick[sample].astype(jnp.float32).reshape(NBLK, BLOCK) * (1.0 - fade)
        trans = trans * fade
    return color.reshape(PIX), trans.reshape(PIX)


def composite(colors, transes, order, axis):
    shape = colors.shape[:axis] + colors.shape[axis + 1:]

    def step(k, carry):
        total, remain = carry
        index = order[k]
        color = lax.dynamic_index_in_dim(colors, index, axis, False)
        trans = lax.dynamic_index_in_dim(transes, index, axis, False)
        return (total + remain * color, remain * trans)

    start = (jnp.zeros(shape, jnp.float32), jnp.ones(shape, jnp.float32))
    return lax.fori_loop(0, order.shape[0], step, start)


def reference(density, source, occupancy, row_order, col_order):
    def column(index):
        dens_column = lax.dynamic_index_in_dim(density, index, 0, False)
        src_column = lax.dynamic_index_in_dim(source, index, 0, False)
        occ_column = lax.dynamic_index_in_dim(occupancy, index, 0, False)
        colors, transes = lax.map(lambda items: shade_brick(items[0], items[1], items[2]), (dens_column, src_column, occ_column))
        return composite(colors, transes, row_order, 0)

    def step(k, carry):
        total, remain = carry
        color, trans = column(col_order[k])
        return (total + remain * color, remain * trans)

    start = (jnp.zeros((PIX,), jnp.float32), jnp.ones((PIX,), jnp.float32))
    emission, transmittance = lax.fori_loop(0, N_GX, step, start)
    return emission, transmittance
```

```python
import functools

import jax
import jax.numpy as jnp
from jax import lax
from jax.experimental import pallas as pl
from jax.experimental.pallas import tpu as pltpu
from jax.sharding import PartitionSpec as P

MESH = pl.DeviceIdType.MESH
ROWS = 16
COLS = 32
DEPTH = 8
BLOCK = 128
NBLK = 1024
PIX = NBLK * BLOCK
FOOT = 102
GROUP = NBLK // COLS
CHUNKS = 4


def kernel(
    dens_hbm,
    src_hbm,
    occ_ref,
    row_ref,
    col_ref,
    emission_ref,
    transmittance_ref,
    dens,
    src,
    dens_rows,
    src_rows,
    occ_rows,
    send1,
    recv1,
    info,
    recv_info,
    send2,
    recv2,
    load_sem,
    send_sems,
    recv_sems,
):
    gx = lax.axis_index("gx")
    gy = lax.axis_index("gy")

    width = NBLK // CHUNKS
    for part in range(CHUNKS):
        cut = pl.ds(part * width, width)
        pltpu.make_async_copy(dens_hbm.at[cut], dens.at[cut], load_sem.at[0]).start()
        pltpu.make_async_copy(src_hbm.at[cut], src.at[cut], load_sem.at[1]).start()

    barrier = pltpu.get_barrier_semaphore()

    @pl.loop(1, ROWS)
    def _(d):
        pl.semaphore_signal(
            barrier, inc=1, device_id={"gy": lax.rem(gy + d, ROWS)}, device_id_type=MESH
        )

    @pl.loop(1, COLS)
    def _(d):
        pl.semaphore_signal(
            barrier, inc=1, device_id={"gx": lax.rem(gx + d, COLS)}, device_id_type=MESH
        )

    occ = occ_ref[0]
    index = lax.broadcasted_iota(jnp.int32, (1, NBLK), 1)
    far = jnp.int32(4 * NBLK)
    low = jnp.min(jnp.where(occ > 0, index, far))
    high = jnp.min(jnp.where((occ > 0) & (index >= NBLK // 2), index, far))
    start = jnp.where((low < FOOT) & (high < far), high, low)
    pair = start >> 1
    info[...] = jnp.full((1, BLOCK), pair, jnp.int32)
    recv_info[gy] = jnp.full((1, BLOCK), pair, jnp.int32)

    def group_of(first, j, t):
        begin = (first - j + 15) >> 4
        return (t + 4 * ((begin - t + 3) >> 2)) & (COLS - 1)

    row = lax.broadcasted_iota(jnp.int32, (8, NBLK), 0)
    lane = lax.broadcasted_iota(jnp.int32, (8, NBLK), 1)
    occ_all = jnp.broadcast_to(occ.astype(jnp.float32), (8, NBLK))

    @pl.loop(0, ROWS)
    def _(j):
        block = group_of(pair, j, row >> 1) * GROUP + 2 * j + (row & 1)
        mine = jnp.sum(jnp.where(lane == block, occ_all, 0.0), axis=1, keepdims=True)
        occ_rows[j] = jnp.broadcast_to(mine, (8, BLOCK))

    pl.semaphore_wait(barrier, ROWS - 1 + COLS - 1)

    @pl.loop(1, ROWS)
    def _(d):
        pltpu.make_async_remote_copy(
            src_ref=info,
            dst_ref=recv_info.at[gy],
            send_sem=send_sems.at[0],
            recv_sem=recv_sems.at[0],
            device_id={"gy": lax.rem(gy + d, ROWS)},
            device_id_type=MESH,
        ).start()

    pltpu.make_async_copy(dens, dens, load_sem.at[0]).wait()
    pltpu.make_async_copy(src, src, load_sem.at[1]).wait()

    def shade(j):
        for t in range(4):
            group = group_of(pair, j, t)
            for h in range(2):
                k = 2 * t + h
                block = group * GROUP + 2 * j + h
                to = pl.ds(pl.multiple_of(j * 64 + k * 8, 8), 8)
                dens_rows[to, :] = dens[block].astype(jnp.float32)
                src_rows[to, :] = src[block].astype(jnp.float32)
        occupied = occ_rows[j]
        color = jnp.zeros((8, BLOCK), jnp.float32)
        trans = jnp.ones((8, BLOCK), jnp.float32)
        for s in range(DEPTH):
            cut = pl.ds(j * 64 + s, 8, stride=8)
            fade = jnp.exp(-(dens_rows[cut, :] * occupied))
            color = color + trans * src_rows[cut, :] * (1.0 - fade)
            trans = trans * fade
        return color, trans

    @pl.loop(1, ROWS)
    def _(d):
        j = lax.rem(gy + d, ROWS)
        color, trans = shade(j)
        send1[j, 0] = color
        send1[j, 1] = trans
        pltpu.make_async_remote_copy(
            src_ref=send1.at[j],
            dst_ref=recv1.at[gy],
            send_sem=send_sems.at[1],
            recv_sem=recv_sems.at[1],
            device_id={"gy": j},
            device_id_type=MESH,
        ).start()

    color, trans = shade(gy)
    recv1[gy, 0] = color
    recv1[gy, 1] = trans

    others = recv_info.at[pl.ds(0, ROWS - 1)]
    pltpu.make_async_copy(others, others, recv_sems.at[0]).wait()
    others = recv1.at[pl.ds(0, ROWS - 1)]
    pltpu.make_async_copy(others, others, recv_sems.at[1]).wait()

    t_of = lax.broadcasted_iota(jnp.int32, (8, BLOCK), 0) >> 1

    def over_row(k, carry):
        total, remain = carry
        r = row_ref[k]
        color = recv1[r, 0]
        trans = recv1[r, 1]
        first = jnp.broadcast_to(recv_info[r], (8, BLOCK))
        place = group_of(first, gy, t_of) >> 2
        new_total, new_remain = [], []
        for v in range(8):
            here = place == v
            new_total.append(total[v] + remain[v] * jnp.where(here, color, 0.0))
            new_remain.append(remain[v] * jnp.where(here, trans, 1.0))
        return tuple(new_total), tuple(new_remain)

    zeros = tuple(jnp.zeros((8, BLOCK), jnp.float32) for _ in range(8))
    ones = tuple(jnp.ones((8, BLOCK), jnp.float32) for _ in range(8))
    total, remain = lax.fori_loop(0, ROWS, over_row, (zeros, ones))
    for v in range(8):
        for t in range(4):
            send2[4 * v + t, 0] = total[v][2 * t : 2 * t + 2]
            send2[4 * v + t, 1] = remain[v][2 * t : 2 * t + 2]

    @pl.loop(1, COLS)
    def _(d):
        i = lax.rem(gx + d, COLS)
        pltpu.make_async_remote_copy(
            src_ref=send2.at[i],
            dst_ref=recv2.at[gx],
            send_sem=send_sems.at[2],
            recv_sem=recv_sems.at[2],
            device_id={"gx": i},
            device_id_type=MESH,
        ).start()

    recv2[gx] = send2[gx]
    others2 = recv2.at[pl.ds(0, COLS - 1)]
    pltpu.make_async_copy(others2, others2, recv_sems.at[2]).wait()

    def over_column(k, carry):
        total, remain = carry
        c = col_ref[k]
        return total + remain * recv2[c, 0], remain * recv2[c, 1]

    total, remain = lax.fori_loop(
        0,
        COLS,
        over_column,
        (jnp.zeros((2, BLOCK), jnp.float32), jnp.ones((2, BLOCK), jnp.float32)),
    )
    emission_ref[...] = total
    transmittance_ref[...] = remain

    others = recv_info.at[pl.ds(0, ROWS - 1)]
    pltpu.make_async_copy(others, others, send_sems.at[0]).wait()
    others = recv1.at[pl.ds(0, ROWS - 1)]
    pltpu.make_async_copy(others, others, send_sems.at[1]).wait()
    pltpu.make_async_copy(others2, others2, send_sems.at[2]).wait()


def on_device(density, source, occupancy, row_order, col_order):
    vmem = pl.BlockSpec(memory_space=pltpu.VMEM)
    smem = pl.BlockSpec(memory_space=pltpu.SMEM)
    hbm = pl.BlockSpec(memory_space=pltpu.HBM)
    out = jax.ShapeDtypeStruct((2, BLOCK), jnp.float32)
    density, source = (
        a.reshape(DEPTH, NBLK, BLOCK).transpose(1, 0, 2) for a in (density, source)
    )
    emission, transmittance = pl.pallas_call(
        kernel,
        out_shape=(out, out),
        in_specs=[hbm, hbm, vmem, smem, smem],
        out_specs=(vmem, vmem),
        scratch_shapes=[
            pltpu.VMEM((NBLK, DEPTH, BLOCK), jnp.bfloat16),
            pltpu.VMEM((NBLK, DEPTH, BLOCK), jnp.bfloat16),
            pltpu.VMEM((ROWS * 64, BLOCK), jnp.float32),
            pltpu.VMEM((ROWS * 64, BLOCK), jnp.float32),
            pltpu.VMEM((ROWS, 8, BLOCK), jnp.float32),
            pltpu.VMEM((ROWS, 2, 8, BLOCK), jnp.float32),
            pltpu.VMEM((ROWS, 2, 8, BLOCK), jnp.float32),
            pltpu.VMEM((1, BLOCK), jnp.int32),
            pltpu.VMEM((ROWS, 1, BLOCK), jnp.int32),
            pltpu.VMEM((COLS, 2, 2, BLOCK), jnp.float32),
            pltpu.VMEM((COLS, 2, 2, BLOCK), jnp.float32),
            pltpu.SemaphoreType.DMA((2,)),
            pltpu.SemaphoreType.DMA((3,)),
            pltpu.SemaphoreType.DMA((3,)),
        ],
        compiler_params=pltpu.CompilerParams(
            collective_id=0, has_side_effects=True, vmem_limit_bytes=60 * 1024 * 1024
        ),
    )(density, source, occupancy, row_order, col_order)
    return emission.reshape(2 * BLOCK), transmittance.reshape(2 * BLOCK)


def solution(mesh):
    placed = (P("gx", "gy", None, None), P("gx", "gy", None, None), P("gx", "gy", None), P(), P())
    return jax.shard_map(
        on_device,
        mesh=mesh,
        in_specs=placed,
        out_specs=(P(("gx", "gy")), P(("gx", "gy"))),
        check_vma=False,
    )
```

```python
import functools

import jax
import jax.numpy as jnp
from jax import lax
from jax.experimental import pallas as pl
from jax.experimental.pallas import tpu as pltpu
from jax.sharding import PartitionSpec as P

MESH = pl.DeviceIdType.MESH
ROWS = 16
COLS = 32
DEPTH = 8
BLOCK = 128
NBLK = 1024
PIX = NBLK * BLOCK
FOOT = 102
GROUP = NBLK // COLS


def peer(me, d):
    chip = d >> 1
    away = ROWS // 4 + jnp.where(chip % 2 == 0, -(chip >> 1), (chip + 1) >> 1)
    return lax.rem((me ^ (1 - (d & 1))) + 2 * away, ROWS)


def kernel(
    dens_hbm,
    src_hbm,
    occ_hbm,
    row_hbm,
    col_hbm,
    out_ref,
    occ_ref,
    row_ref,
    col_ref,
    dens,
    src,
    dens_rows,
    src_rows,
    occ_rows,
    send1,
    recv1,
    info,
    recv_info,
    send2,
    recv2,
    load_sem,
    send_sems,
    recv_sems,
):
    gx = lax.axis_index("gx")
    gy = lax.axis_index("gy")

    barrier = pltpu.get_barrier_semaphore()

    @pl.loop(1, COLS)
    def _(d):
        pl.semaphore_signal(
            barrier, inc=1, device_id={"gx": lax.rem(gx + d, COLS)}, device_id_type=MESH
        )

    @pl.loop(1, ROWS)
    def _(d):
        pl.semaphore_signal(
            barrier, inc=1, device_id={"gy": lax.rem(gy + d, ROWS)}, device_id_type=MESH
        )

    small = [
        pltpu.make_async_copy(occ_hbm, occ_ref, load_sem.at[2]),
        pltpu.make_async_copy(row_hbm, row_ref, load_sem.at[3]),
        pltpu.make_async_copy(col_hbm, col_ref, load_sem.at[4]),
    ]
    large = [
        pltpu.make_async_copy(dens_hbm, dens, load_sem.at[0]),
        pltpu.make_async_copy(src_hbm, src, load_sem.at[1]),
    ]
    for copy in small + large:
        copy.start()

    small[0].wait()

    occ = occ_ref[0]
    index = lax.broadcasted_iota(jnp.int32, (1, NBLK), 1)
    far = jnp.int32(4 * NBLK)
    low = jnp.min(jnp.where(occ > 0, index, far))
    high = jnp.min(jnp.where((occ > 0) & (index >= NBLK // 2), index, far))
    start = jnp.where((low < FOOT) & (high < far), high, low)
    pair = start >> 1
    info[...] = jnp.full((1, BLOCK), pair, jnp.int32)
    recv_info[gy] = jnp.full((1, BLOCK), pair, jnp.int32)

    def group_of(first, j, t):
        begin = (first - j + 15) >> 4
        return (t + 4 * ((begin - t + 3) >> 2)) & (COLS - 1)

    row = lax.broadcasted_iota(jnp.int32, (8, NBLK), 0)
    lane = lax.broadcasted_iota(jnp.int32, (8, NBLK), 1)
    occ_all = jnp.broadcast_to(occ.astype(jnp.float32), (8, NBLK))

    @pl.loop(0, ROWS)
    def _(j):
        block = group_of(pair, j, row >> 1) * GROUP + 2 * j + (row & 1)
        mine = jnp.sum(jnp.where(lane == block, occ_all, 0.0), axis=1, keepdims=True)
        occ_rows[j] = jnp.broadcast_to(mine, (8, BLOCK))

    pl.semaphore_wait(barrier, ROWS - 1 + COLS - 1)

    @pl.loop(0, ROWS - 1)
    def _(d):
        pltpu.make_async_remote_copy(
            src_ref=info,
            dst_ref=recv_info.at[gy],
            send_sem=send_sems.at[0],
            recv_sem=recv_sems.at[0],
            device_id={"gy": peer(gy, d)},
            device_id_type=MESH,
        ).start()

    for copy in large:
        copy.wait()

    def shade(j):
        for t in range(4):
            group = group_of(pair, j, t)
            for h in range(2):
                k = 2 * t + h
                block = group * GROUP + 2 * j + h
                to = pl.ds(pl.multiple_of(j * 64 + k * 8, 8), 8)
                dens_rows[to, :] = dens[block].astype(jnp.float32)
                src_rows[to, :] = src[block].astype(jnp.float32)
        occupied = occ_rows[j]
        color = jnp.zeros((8, BLOCK), jnp.float32)
        trans = jnp.ones((8, BLOCK), jnp.float32)
        for s in range(DEPTH):
            cut = pl.ds(j * 64 + s, 8, stride=8)
            fade = jnp.exp(-(dens_rows[cut, :] * occupied))
            color = color + trans * src_rows[cut, :] * (1.0 - fade)
            trans = trans * fade
        return color, trans

    @pl.loop(0, ROWS - 1)
    def _(d):
        j = peer(gy, d)
        color, trans = shade(j)
        send1[j, 0] = color
        send1[j, 1] = trans
        pltpu.make_async_remote_copy(
            src_ref=send1.at[j],
            dst_ref=recv1.at[gy],
            send_sem=send_sems.at[1],
            recv_sem=recv_sems.at[1],
            device_id={"gy": j},
            device_id_type=MESH,
        ).start()

    color, trans = shade(gy)
    recv1[gy, 0] = color
    recv1[gy, 1] = trans

    others = recv_info.at[pl.ds(0, ROWS - 1)]
    pltpu.make_async_copy(others, others, recv_sems.at[0]).wait()
    others = recv1.at[pl.ds(0, ROWS - 1)]
    pltpu.make_async_copy(others, others, recv_sems.at[1]).wait()

    small[1].wait()
    small[2].wait()

    t_of = lax.broadcasted_iota(jnp.int32, (8, BLOCK), 0) >> 1

    def over_row(k, carry):
        total, remain = carry
        r = row_ref[k]
        color = recv1[r, 0]
        trans = recv1[r, 1]
        first = jnp.broadcast_to(recv_info[r], (8, BLOCK))
        place = group_of(first, gy, t_of) >> 2
        new_total, new_remain = [], []
        for v in range(8):
            here = place == v
            new_total.append(total[v] + remain[v] * jnp.where(here, color, 0.0))
            new_remain.append(remain[v] * jnp.where(here, trans, 1.0))
        return tuple(new_total), tuple(new_remain)

    zeros = tuple(jnp.zeros((8, BLOCK), jnp.float32) for _ in range(8))
    ones = tuple(jnp.ones((8, BLOCK), jnp.float32) for _ in range(8))
    total, remain = lax.fori_loop(0, ROWS, over_row, (zeros, ones), unroll=4)
    for v in range(8):
        for t in range(4):
            send2[4 * v + t, 0] = total[v][2 * t : 2 * t + 2]
            send2[4 * v + t, 1] = remain[v][2 * t : 2 * t + 2]

    @pl.loop(1, COLS)
    def _(d):
        i = lax.rem(gx + d, COLS)
        pltpu.make_async_remote_copy(
            src_ref=send2.at[i],
            dst_ref=recv2.at[gx],
            send_sem=send_sems.at[2],
            recv_sem=recv_sems.at[2],
            device_id={"gx": i},
            device_id_type=MESH,
        ).start()

    recv2[gx] = send2[gx]
    others2 = recv2.at[pl.ds(0, COLS - 1)]
    pltpu.make_async_copy(others2, others2, recv_sems.at[2]).wait()

    def over_column(k, carry):
        total, remain = carry
        c = col_ref[k]
        return total + remain * recv2[c, 0], remain * recv2[c, 1]

    total, remain = lax.fori_loop(
        0,
        COLS,
        over_column,
        (jnp.zeros((2, BLOCK), jnp.float32), jnp.ones((2, BLOCK), jnp.float32)),
        unroll=8,
    )
    out_ref[0] = total
    out_ref[1] = remain

    others = recv_info.at[pl.ds(0, ROWS - 1)]
    pltpu.make_async_copy(others, others, send_sems.at[0]).wait()
    others = recv1.at[pl.ds(0, ROWS - 1)]
    pltpu.make_async_copy(others, others, send_sems.at[1]).wait()
    pltpu.make_async_copy(others2, others2, send_sems.at[2]).wait()


def deliver(both_ref, emission_ref, transmittance_ref):
    emission_ref[...] = both_ref[0]
    transmittance_ref[...] = both_ref[1]


def on_device(density, source, occupancy, row_order, col_order):
    vmem = pl.BlockSpec(memory_space=pltpu.VMEM)
    hbm = pl.BlockSpec(memory_space=pltpu.HBM)
    density, source = (
        a.reshape(DEPTH, NBLK, BLOCK).transpose(1, 0, 2) for a in (density, source)
    )
    both = pl.pallas_call(
        kernel,
        out_shape=jax.ShapeDtypeStruct((2, 2, BLOCK), jnp.float32),
        in_specs=[hbm] * 5,
        out_specs=vmem,
        scratch_shapes=[
            pltpu.VMEM((1, 1, NBLK), jnp.int32),
            pltpu.SMEM((ROWS,), jnp.int32),
            pltpu.SMEM((COLS,), jnp.int32),
            pltpu.VMEM((NBLK, DEPTH, BLOCK), jnp.bfloat16),
            pltpu.VMEM((NBLK, DEPTH, BLOCK), jnp.bfloat16),
            pltpu.VMEM((ROWS * 64, BLOCK), jnp.float32),
            pltpu.VMEM((ROWS * 64, BLOCK), jnp.float32),
            pltpu.VMEM((ROWS, 8, BLOCK), jnp.float32),
            pltpu.VMEM((ROWS, 2, 8, BLOCK), jnp.float32),
            pltpu.VMEM((ROWS, 2, 8, BLOCK), jnp.float32),
            pltpu.VMEM((1, BLOCK), jnp.int32),
            pltpu.VMEM((ROWS, 1, BLOCK), jnp.int32),
            pltpu.VMEM((COLS, 2, 2, BLOCK), jnp.float32),
            pltpu.VMEM((COLS, 2, 2, BLOCK), jnp.float32),
            pltpu.SemaphoreType.DMA((5,)),
            pltpu.SemaphoreType.DMA((3,)),
            pltpu.SemaphoreType.DMA((3,)),
        ],
        compiler_params=pltpu.CompilerParams(
            collective_id=0, has_side_effects=True, vmem_limit_bytes=60 * 1024 * 1024
        ),
    )(density, source, occupancy, row_order, col_order)
    out = jax.ShapeDtypeStruct((2, BLOCK), jnp.float32)
    emission, transmittance = pl.pallas_call(
        deliver, out_shape=(out, out), in_specs=[vmem], out_specs=(vmem, vmem)
    )(both)
    return emission.reshape(2 * BLOCK), transmittance.reshape(2 * BLOCK)


def solution(mesh):
    placed = (P("gx", "gy", None, None), P("gx", "gy", None, None), P("gx", "gy", None), P(), P())
    return jax.shard_map(
        on_device,
        mesh=mesh,
        in_specs=placed,
        out_specs=(P(("gx", "gy")), P(("gx", "gy"))),
        check_vma=False,
    )
```

```python
import functools

import jax
import jax.numpy as jnp
from jax import lax
from jax.experimental import pallas as pl
from jax.experimental.pallas import tpu as pltpu
from jax.sharding import PartitionSpec as P

MESH = pl.DeviceIdType.MESH
ROWS = 16
COLS = 32
DEPTH = 8
BLOCK = 128
NBLK = 1024
PIX = NBLK * BLOCK
FOOT = 102
GROUP = NBLK // COLS


def peer(me, d):
    chip = d >> 1
    away = ROWS // 4 + jnp.where(chip % 2 == 0, -(chip >> 1), (chip + 1) >> 1)
    return lax.rem((me ^ (1 - (d & 1))) + 2 * away, ROWS)


def column_peer(me, d):
    turn, dy = d & 3, d >> 2
    dx = jnp.where(turn < 2, 2 - turn, 9 - 3 * turn)
    dy = 4 + jnp.where(dy % 2 == 0, -(dy >> 1), (dy + 1) >> 1)
    return ((((me >> 3) + dx) & 3) << 3) + (((me & 7) + dy) & 7)


def kernel(
    dens_hbm,
    src_hbm,
    occ_hbm,
    row_hbm,
    col_hbm,
    out_ref,
    occ_ref,
    row_ref,
    col_ref,
    dens,
    src,
    dens_rows,
    src_rows,
    occ_rows,
    send1,
    recv1,
    info,
    recv_info,
    send2,
    recv2,
    load_sem,
    send_sems,
    recv_sems,
):
    gx = lax.axis_index("gx")
    gy = lax.axis_index("gy")

    small = [
        pltpu.make_async_copy(occ_hbm, occ_ref, load_sem.at[2]),
        pltpu.make_async_copy(row_hbm, row_ref, load_sem.at[3]),
        pltpu.make_async_copy(col_hbm, col_ref, load_sem.at[4]),
    ]
    large = [
        pltpu.make_async_copy(dens_hbm, dens, load_sem.at[0]),
        pltpu.make_async_copy(src_hbm, src, load_sem.at[1]),
    ]
    for copy in small + large:
        copy.start()

    barrier = pltpu.get_barrier_semaphore()

    @pl.loop(1, COLS)
    def _(d):
        pl.semaphore_signal(
            barrier, inc=1, device_id={"gx": lax.rem(gx + d, COLS)}, device_id_type=MESH
        )

    @pl.loop(1, ROWS)
    def _(d):
        pl.semaphore_signal(
            barrier, inc=1, device_id={"gy": lax.rem(gy + d, ROWS)}, device_id_type=MESH
        )

    small[0].wait()

    occ = occ_ref[0]
    index = lax.broadcasted_iota(jnp.int32, (1, NBLK), 1)
    far = jnp.int32(4 * NBLK)
    low = jnp.min(jnp.where(occ > 0, index, far))
    high = jnp.min(jnp.where((occ > 0) & (index >= NBLK // 2), index, far))
    start = jnp.where((low < FOOT) & (high < far), high, low)
    pair = start >> 1
    info[...] = jnp.full((1, BLOCK), pair, jnp.int32)
    recv_info[gy] = jnp.full((1, BLOCK), pair, jnp.int32)

    def group_of(first, j, t):
        begin = (first - j + 15) >> 4
        return (t + 4 * ((begin - t + 3) >> 2)) & (COLS - 1)

    row = lax.broadcasted_iota(jnp.int32, (8, BLOCK), 0)
    lane = lax.broadcasted_iota(jnp.int32, (8, BLOCK), 1)
    occ_parts = [
        jnp.broadcast_to(occ[:, c : c + BLOCK], (8, BLOCK)).astype(jnp.float32)
        for c in range(0, NBLK, BLOCK)
    ]

    @pl.loop(0, ROWS, unroll=4)
    def _(j):
        block = group_of(pair, j, row >> 1) * GROUP + 2 * j + (row & 1)
        mine = jnp.zeros((8, BLOCK), jnp.float32)
        for c, part in enumerate(occ_parts):
            mine = mine + jnp.where(lane == block - c * BLOCK, part, 0.0)
        mine = jnp.sum(mine, axis=1, keepdims=True)
        occ_rows[j] = jnp.broadcast_to(mine, (8, BLOCK))

    pl.semaphore_wait(barrier, ROWS - 1 + COLS - 1)

    @pl.loop(0, ROWS - 1)
    def _(d):
        pltpu.make_async_remote_copy(
            src_ref=info,
            dst_ref=recv_info.at[gy],
            send_sem=send_sems.at[0],
            recv_sem=recv_sems.at[0],
            device_id={"gy": peer(gy, d)},
            device_id_type=MESH,
        ).start()

    for copy in large:
        copy.wait()

    def shade(j):
        for t in range(4):
            group = group_of(pair, j, t)
            for h in range(2):
                k = 2 * t + h
                block = group * GROUP + 2 * j + h
                to = pl.ds(pl.multiple_of(j * 64 + k * 8, 8), 8)
                dens_rows[to, :] = dens[block].astype(jnp.float32)
                src_rows[to, :] = src[block].astype(jnp.float32)
        occupied = occ_rows[j]
        color = jnp.zeros((8, BLOCK), jnp.float32)
        trans = jnp.ones((8, BLOCK), jnp.float32)
        for s in range(DEPTH):
            cut = pl.ds(j * 64 + s, 8, stride=8)
            fade = jnp.exp(-(dens_rows[cut, :] * occupied))
            color = color + trans * src_rows[cut, :] * (1.0 - fade)
            trans = trans * fade
        return color, trans

    @pl.loop(0, ROWS - 1)
    def _(d):
        j = peer(gy, d)
        color, trans = shade(j)
        send1[j, 0] = color
        send1[j, 1] = trans
        pltpu.make_async_remote_copy(
            src_ref=send1.at[j],
            dst_ref=recv1.at[gy],
            send_sem=send_sems.at[1],
            recv_sem=recv_sems.at[1],
            device_id={"gy": j},
            device_id_type=MESH,
        ).start()

    color, trans = shade(gy)
    recv1[gy, 0] = color
    recv1[gy, 1] = trans

    others = recv_info.at[pl.ds(0, ROWS - 1)]
    pltpu.make_async_copy(others, others, recv_sems.at[0]).wait()
    others = recv1.at[pl.ds(0, ROWS - 1)]
    pltpu.make_async_copy(others, others, recv_sems.at[1]).wait()

    small[1].wait()
    small[2].wait()

    t_of = lax.broadcasted_iota(jnp.int32, (8, BLOCK), 0) >> 1

    def over_row(k, carry):
        total, remain = carry
        r = row_ref[k]
        color = recv1[r, 0]
        trans = recv1[r, 1]
        first = jnp.broadcast_to(recv_info[r], (8, BLOCK))
        place = group_of(first, gy, t_of) >> 2
        new_total, new_remain = [], []
        for v in range(8):
            here = place == v
            new_total.append(total[v] + remain[v] * jnp.where(here, color, 0.0))
            new_remain.append(remain[v] * jnp.where(here, trans, 1.0))
        return tuple(new_total), tuple(new_remain)

    zeros = tuple(jnp.zeros((8, BLOCK), jnp.float32) for _ in range(8))
    ones = tuple(jnp.ones((8, BLOCK), jnp.float32) for _ in range(8))
    total, remain = lax.fori_loop(0, ROWS, over_row, (zeros, ones), unroll=4)
    for v in range(8):
        for t in range(4):
            send2[4 * v + t, 0] = total[v][2 * t : 2 * t + 2]
            send2[4 * v + t, 1] = remain[v][2 * t : 2 * t + 2]

    @pl.loop(0, COLS - 1)
    def _(d):
        i = column_peer(gx, d)
        pltpu.make_async_remote_copy(
            src_ref=send2.at[i],
            dst_ref=recv2.at[gx],
            send_sem=send_sems.at[2],
            recv_sem=recv_sems.at[2],
            device_id={"gx": i},
            device_id_type=MESH,
        ).start()

    recv2[gx] = send2[gx]
    others2 = recv2.at[pl.ds(0, COLS - 1)]
    pltpu.make_async_copy(others2, others2, recv_sems.at[2]).wait()

    def over_column(k, carry):
        total, remain = carry
        c = col_ref[k]
        return total + remain * recv2[c, 0], remain * recv2[c, 1]

    total, remain = lax.fori_loop(
        0,
        COLS,
        over_column,
        (jnp.zeros((2, BLOCK), jnp.float32), jnp.ones((2, BLOCK), jnp.float32)),
        unroll=8,
    )
    out_ref[0] = total
    out_ref[1] = remain

    others = recv_info.at[pl.ds(0, ROWS - 1)]
    pltpu.make_async_copy(others, others, send_sems.at[0]).wait()
    others = recv1.at[pl.ds(0, ROWS - 1)]
    pltpu.make_async_copy(others, others, send_sems.at[1]).wait()
    pltpu.make_async_copy(others2, others2, send_sems.at[2]).wait()


def deliver(both_ref, emission_ref, transmittance_ref):
    emission_ref[...] = both_ref[0]
    transmittance_ref[...] = both_ref[1]


def on_device(density, source, occupancy, row_order, col_order):
    vmem = pl.BlockSpec(memory_space=pltpu.VMEM)
    hbm = pl.BlockSpec(memory_space=pltpu.HBM)
    density, source = (
        a.reshape(DEPTH, NBLK, BLOCK).transpose(1, 0, 2) for a in (density, source)
    )
    operands = [
        pltpu.with_memory_space_constraint(a, pltpu.HBM)
        for a in (density, source, occupancy, row_order, col_order)
    ]
    both = pl.pallas_call(
        kernel,
        out_shape=pltpu.VMEM((2, 2, BLOCK), jnp.float32),
        in_specs=[hbm] * 5,
        out_specs=vmem,
        scratch_shapes=[
            pltpu.VMEM((1, 1, NBLK), jnp.int32),
            pltpu.SMEM((ROWS,), jnp.int32),
            pltpu.SMEM((COLS,), jnp.int32),
            pltpu.VMEM((NBLK, DEPTH, BLOCK), jnp.bfloat16),
            pltpu.VMEM((NBLK, DEPTH, BLOCK), jnp.bfloat16),
            pltpu.VMEM((ROWS * 64, BLOCK), jnp.float32),
            pltpu.VMEM((ROWS * 64, BLOCK), jnp.float32),
            pltpu.VMEM((ROWS, 8, BLOCK), jnp.float32),
            pltpu.VMEM((ROWS, 2, 8, BLOCK), jnp.float32),
            pltpu.VMEM((ROWS, 2, 8, BLOCK), jnp.float32),
            pltpu.VMEM((1, BLOCK), jnp.int32),
            pltpu.VMEM((ROWS, 1, BLOCK), jnp.int32),
            pltpu.VMEM((COLS, 2, 2, BLOCK), jnp.float32),
            pltpu.VMEM((COLS, 2, 2, BLOCK), jnp.float32),
            pltpu.SemaphoreType.DMA((5,)),
            pltpu.SemaphoreType.DMA((3,)),
            pltpu.SemaphoreType.DMA((3,)),
        ],
        compiler_params=pltpu.CompilerParams(
            collective_id=0, has_side_effects=True, vmem_limit_bytes=40 * 1024 * 1024
        ),
    )(*operands)
    out = jax.ShapeDtypeStruct((2, BLOCK), jnp.float32)
    emission, transmittance = pl.pallas_call(
        deliver,
        out_shape=(out, out),
        in_specs=[vmem],
        out_specs=(vmem, vmem),
        compiler_params=pltpu.CompilerParams(vmem_limit_bytes=2**20),
    )(both)
    return emission.reshape(2 * BLOCK), transmittance.reshape(2 * BLOCK)


def solution(mesh):
    placed = (P("gx", "gy", None, None), P("gx", "gy", None, None), P("gx", "gy", None), P(), P())
    return jax.shard_map(
        on_device,
        mesh=mesh,
        in_specs=placed,
        out_specs=(P(("gx", "gy")), P(("gx", "gy"))),
        check_vma=False,
    )
```

```python
import functools

import jax
import jax.numpy as jnp
from jax import lax
from jax.experimental import pallas as pl
from jax.experimental.pallas import tpu as pltpu
from jax.sharding import PartitionSpec as P

MESH = pl.DeviceIdType.MESH
ROWS = 16
COLS = 32
HALF = ROWS // 2
DEPTH = 8
BLOCK = 128
NBLK = 1024
PIX = NBLK * BLOCK
FOOT = 102
GROUP = NBLK // COLS


def column_peer(me, d):
    turn, dy = d & 3, d >> 2
    dx = jnp.where(turn < 2, 2 - turn, 9 - 3 * turn)
    dy = 4 + jnp.where(dy % 2 == 0, -(dy >> 1), (dy + 1) >> 1)
    return ((((me >> 3) + dx) & 3) << 3) + (((me & 7) + dy) & 7)


def kernel(
    dens_hbm,
    src_hbm,
    occ_hbm,
    row_hbm,
    col_hbm,
    out_ref,
    occ_ref,
    row_ref,
    col_ref,
    dens,
    src,
    dens_rows,
    src_rows,
    occ_rows,
    send1,
    recv1,
    info,
    recv_info,
    send2,
    recv2,
    load_sem,
    send_sems,
    recv_sems,
    late_sem,
    go_sem,
):
    gx = lax.axis_index("gx")
    gy = lax.axis_index("gy")

    barrier = pltpu.get_barrier_semaphore()

    @pl.when(gy < HALF)
    def _():
        @pl.loop(1, ROWS)
        def _(d):
            pl.semaphore_signal(
                barrier, inc=1, device_id={"gy": lax.rem(gy + d, ROWS)}, device_id_type=MESH
            )

    small = [
        pltpu.make_async_copy(occ_hbm, occ_ref, load_sem.at[2]),
        pltpu.make_async_copy(row_hbm, row_ref, load_sem.at[3]),
        pltpu.make_async_copy(col_hbm, col_ref, load_sem.at[4]),
    ]
    large = [
        pltpu.make_async_copy(dens_hbm, dens, load_sem.at[0]),
        pltpu.make_async_copy(src_hbm, src, load_sem.at[1]),
    ]
    for copy in small + large:
        copy.start()

    @pl.loop(0, COLS - 1)
    def _(d):
        pl.semaphore_signal(
            barrier, inc=1, device_id={"gx": column_peer(gx, d)}, device_id_type=MESH
        )

    small[0].wait()

    occ = occ_ref[0]
    index = lax.broadcasted_iota(jnp.int32, (1, NBLK), 1)
    far = jnp.int32(4 * NBLK)
    low = jnp.min(jnp.where(occ > 0, index, far))
    high = jnp.min(jnp.where((occ > 0) & (index >= NBLK // 2), index, far))
    start = jnp.where((low < FOOT) & (high < far), high, low)
    pair = start >> 1
    info[...] = jnp.full((1, BLOCK), pair, jnp.int32)
    recv_info[gy] = jnp.full((1, BLOCK), pair, jnp.int32)

    def group_of(first, j, t):
        begin = (first - j + 15) >> 4
        return (t + 4 * ((begin - t + 3) >> 2)) & (COLS - 1)

    row = lax.broadcasted_iota(jnp.int32, (8, BLOCK), 0)
    lane = lax.broadcasted_iota(jnp.int32, (8, BLOCK), 1)
    occ_parts = [
        jnp.broadcast_to(occ[:, c : c + BLOCK], (8, BLOCK)).astype(jnp.float32)
        for c in range(0, NBLK, BLOCK)
    ]

    @pl.loop(0, ROWS, unroll=4)
    def _(j):
        block = group_of(pair, j, row >> 1) * GROUP + 2 * j + (row & 1)
        mine = jnp.zeros((8, BLOCK), jnp.float32)
        for c, part in enumerate(occ_parts):
            mine = mine + jnp.where(lane == block - c * BLOCK, part, 0.0)
        mine = jnp.sum(mine, axis=1, keepdims=True)
        occ_rows[j] = jnp.broadcast_to(mine, (8, BLOCK))

    pl.semaphore_wait(barrier, COLS - 1 + jnp.where(gy < HALF, HALF - 1, HALF))

    @pl.when(gy >= HALF)
    def _():
        @pl.loop(0, HALF)
        def _(j):
            pl.semaphore_signal(late_sem, inc=1, device_id={"gy": j}, device_id_type=MESH)

    for copy in large:
        copy.wait()

    def shade(j):
        for t in range(4):
            group = group_of(pair, j, t)
            for h in range(2):
                k = 2 * t + h
                block = group * GROUP + 2 * j + h
                to = pl.ds(pl.multiple_of(j * 64 + k * 8, 8), 8)
                dens_rows[to, :] = dens[block].astype(jnp.float32)
                src_rows[to, :] = src[block].astype(jnp.float32)
        occupied = occ_rows[j]
        color = jnp.zeros((8, BLOCK), jnp.float32)
        trans = jnp.ones((8, BLOCK), jnp.float32)
        for s in range(DEPTH):
            cut = pl.ds(j * 64 + s, 8, stride=8)
            fade = jnp.exp(-(dens_rows[cut, :] * occupied))
            color = color + trans * src_rows[cut, :] * (1.0 - fade)
            trans = trans * fade
        return color, trans

    def send(j):
        @pl.when(j != gy)
        def _():
            for part, (ours, theirs) in enumerate(((send1.at[j], recv1), (info, recv_info))):
                pltpu.make_async_remote_copy(
                    src_ref=ours,
                    dst_ref=theirs.at[gy],
                    send_sem=send_sems.at[part],
                    recv_sem=recv_sems.at[part],
                    device_id={"gy": j},
                    device_id_type=MESH,
                ).start()

    def peer(d, half):
        return half * HALF + (lax.rem(gy, HALF) ^ (HALF - 1 - d))

    @pl.loop(0, HALF)
    def _(d):
        j = peer(d, 0)
        color, trans = shade(j)
        send1[j, 0] = color
        send1[j, 1] = trans
        send(j)

    @pl.loop(0, HALF)
    def _(d):
        j = peer(d, 1)
        color, trans = shade(j)
        send1[j, 0] = color
        send1[j, 1] = trans

    @pl.when(gy < HALF)
    def _():
        pl.semaphore_wait(late_sem, HALF)
        pl.semaphore_signal(go_sem, inc=1, device_id={"gy": gy + HALF}, device_id_type=MESH)

    @pl.when(gy >= HALF)
    def _():
        pl.semaphore_wait(go_sem, 1)

    @pl.loop(0, HALF)
    def _(d):
        send(peer(d, 1))

    recv1[gy] = send1[gy]

    for part, ref in enumerate((recv1, recv_info)):
        others = ref.at[pl.ds(0, ROWS - 1)]
        pltpu.make_async_copy(others, others, recv_sems.at[part]).wait()
    small[1].wait()
    small[2].wait()

    t_of = lax.broadcasted_iota(jnp.int32, (8, BLOCK), 0) >> 1

    def over_row(k, carry):
        total, remain = carry
        r = row_ref[k]
        color = recv1[r, 0]
        trans = recv1[r, 1]
        first = jnp.broadcast_to(recv_info[r], (8, BLOCK))
        place = group_of(first, gy, t_of) >> 2
        new_total, new_remain = [], []
        for v in range(8):
            here = place == v
            new_total.append(total[v] + remain[v] * jnp.where(here, color, 0.0))
            new_remain.append(remain[v] * jnp.where(here, trans, 1.0))
        return tuple(new_total), tuple(new_remain)

    zeros = tuple(jnp.zeros((8, BLOCK), jnp.float32) for _ in range(8))
    ones = tuple(jnp.ones((8, BLOCK), jnp.float32) for _ in range(8))
    total, remain = lax.fori_loop(0, ROWS, over_row, (zeros, ones), unroll=4)
    for v in range(8):
        for t in range(4):
            send2[4 * v + t, 0] = total[v][2 * t : 2 * t + 2]
            send2[4 * v + t, 1] = remain[v][2 * t : 2 * t + 2]

    @pl.loop(0, COLS - 1)
    def _(d):
        i = column_peer(gx, d)
        pltpu.make_async_remote_copy(
            src_ref=send2.at[i],
            dst_ref=recv2.at[gx],
            send_sem=send_sems.at[2],
            recv_sem=recv_sems.at[2],
            device_id={"gx": i},
            device_id_type=MESH,
        ).start()

    recv2[gx] = send2[gx]
    others2 = recv2.at[pl.ds(0, COLS - 1)]
    pltpu.make_async_copy(others2, others2, recv_sems.at[2]).wait()

    def over_column(k, carry):
        total, remain = carry
        c = col_ref[k]
        return total + remain * recv2[c, 0], remain * recv2[c, 1]

    total, remain = lax.fori_loop(
        0,
        COLS,
        over_column,
        (jnp.zeros((2, BLOCK), jnp.float32), jnp.ones((2, BLOCK), jnp.float32)),
        unroll=8,
    )
    out_ref[0] = total
    out_ref[1] = remain

    for part, ref in enumerate((recv1, recv_info)):
        others = ref.at[pl.ds(0, ROWS - 1)]
        pltpu.make_async_copy(others, others, send_sems.at[part]).wait()
    pltpu.make_async_copy(others2, others2, send_sems.at[2]).wait()


def deliver(both_ref, emission_ref, transmittance_ref):
    emission_ref[...] = both_ref[0]
    transmittance_ref[...] = both_ref[1]


def on_device(density, source, occupancy, row_order, col_order):
    vmem = pl.BlockSpec(memory_space=pltpu.VMEM)
    hbm = pl.BlockSpec(memory_space=pltpu.HBM)
    density, source = (
        a.reshape(DEPTH, NBLK, BLOCK).transpose(1, 0, 2) for a in (density, source)
    )
    operands = [
        pltpu.with_memory_space_constraint(a, pltpu.HBM)
        for a in (density, source, occupancy, row_order, col_order)
    ]
    both = pl.pallas_call(
        kernel,
        out_shape=pltpu.VMEM((2, 2, BLOCK), jnp.float32),
        in_specs=[hbm] * 5,
        out_specs=vmem,
        scratch_shapes=[
            pltpu.VMEM((1, 1, NBLK), jnp.int32),
            pltpu.SMEM((ROWS,), jnp.int32),
            pltpu.SMEM((COLS,), jnp.int32),
            pltpu.VMEM((NBLK, DEPTH, BLOCK), jnp.bfloat16),
            pltpu.VMEM((NBLK, DEPTH, BLOCK), jnp.bfloat16),
            pltpu.VMEM((ROWS * 64, BLOCK), jnp.float32),
            pltpu.VMEM((ROWS * 64, BLOCK), jnp.float32),
            pltpu.VMEM((ROWS, 8, BLOCK), jnp.float32),
            pltpu.VMEM((ROWS, 2, 8, BLOCK), jnp.float32),
            pltpu.VMEM((ROWS, 2, 8, BLOCK), jnp.float32),
            pltpu.VMEM((1, BLOCK), jnp.int32),
            pltpu.VMEM((ROWS, 1, BLOCK), jnp.int32),
            pltpu.VMEM((COLS, 2, 2, BLOCK), jnp.float32),
            pltpu.VMEM((COLS, 2, 2, BLOCK), jnp.float32),
            pltpu.SemaphoreType.DMA((5,)),
            pltpu.SemaphoreType.DMA((3,)),
            pltpu.SemaphoreType.DMA((3,)),
            pltpu.SemaphoreType.REGULAR,
            pltpu.SemaphoreType.REGULAR,
        ],
        compiler_params=pltpu.CompilerParams(
            collective_id=0, has_side_effects=True, vmem_limit_bytes=40 * 1024 * 1024
        ),
    )(*operands)
    out = jax.ShapeDtypeStruct((2, BLOCK), jnp.float32)
    emission, transmittance = pl.pallas_call(
        deliver,
        out_shape=(out, out),
        in_specs=[vmem],
        out_specs=(vmem, vmem),
        compiler_params=pltpu.CompilerParams(vmem_limit_bytes=2**20),
    )(both)
    return emission.reshape(2 * BLOCK), transmittance.reshape(2 * BLOCK)


def solution(mesh):
    placed = (P("gx", "gy", None, None), P("gx", "gy", None, None), P("gx", "gy", None), P(), P())
    return jax.shard_map(
        on_device,
        mesh=mesh,
        in_specs=placed,
        out_specs=(P(("gx", "gy")), P(("gx", "gy"))),
        check_vma=False,
    )
```

```python
import functools

import jax
import jax.numpy as jnp
from jax import lax
from jax.experimental import pallas as pl
from jax.experimental.pallas import tpu as pltpu
from jax.sharding import PartitionSpec as P

MESH = pl.DeviceIdType.MESH
ROWS = 16
COLS = 32
HALF = ROWS // 2
HUB = 8
DEPTH = 8
BLOCK = 128
NBLK = 1024
PIX = NBLK * BLOCK
FOOT = 102
GROUP = NBLK // COLS


def column_peer(me, d):
    turn, dy = d & 3, d >> 2
    dx = jnp.where(turn < 2, 2 - turn, 9 - 3 * turn)
    dy = 4 + jnp.where(dy % 2 == 0, -(dy >> 1), (dy + 1) >> 1)
    return ((((me >> 3) + dx) & 3) << 3) + (((me & 7) + dy) & 7)


def kernel(
    dens_hbm,
    src_hbm,
    occ_hbm,
    row_hbm,
    col_hbm,
    out_ref,
    occ_ref,
    row_ref,
    col_ref,
    dens,
    src,
    dens_rows,
    src_rows,
    occ_rows,
    send1,
    recv1,
    info,
    recv_info,
    send2,
    recv2,
    load_sem,
    send_sems,
    recv_sems,
    late_sem,
    go_sem,
    row_sem,
    row_go_sem,
):
    gx = lax.axis_index("gx")
    gy = lax.axis_index("gy")

    barrier = pltpu.get_barrier_semaphore()

    small = [
        pltpu.make_async_copy(occ_hbm, occ_ref, load_sem.at[2]),
        pltpu.make_async_copy(row_hbm, row_ref, load_sem.at[3]),
        pltpu.make_async_copy(col_hbm, col_ref, load_sem.at[4]),
    ]
    large = [
        pltpu.make_async_copy(dens_hbm, dens, load_sem.at[0]),
        pltpu.make_async_copy(src_hbm, src, load_sem.at[1]),
    ]
    for copy in small:
        copy.start()
    for at in range(0, NBLK, NBLK // 4):
        cut = pl.ds(at, NBLK // 4)
        pltpu.make_async_copy(dens_hbm.at[cut], dens.at[cut], load_sem.at[0]).start()
        pltpu.make_async_copy(src_hbm.at[cut], src.at[cut], load_sem.at[1]).start()

    @pl.when(gy < HALF)
    def _():
        @pl.loop(1, ROWS)
        def _(d):
            pl.semaphore_signal(
                barrier, inc=1, device_id={"gy": lax.rem(gy + d, ROWS)}, device_id_type=MESH
            )

    @pl.when(gx == HUB)
    def _():
        @pl.loop(1, COLS)
        def _(i):
            pl.semaphore_signal(barrier, inc=1, device_id={"gx": lax.rem(HUB + i, COLS)}, device_id_type=MESH)

    small[0].wait()

    occ = occ_ref[0]
    index = lax.broadcasted_iota(jnp.int32, (1, NBLK), 1)
    far = jnp.int32(4 * NBLK)
    low = jnp.min(jnp.where(occ > 0, index, far))
    high = jnp.min(jnp.where((occ > 0) & (index >= NBLK // 2), index, far))
    start = jnp.where((low < FOOT) & (high < far), high, low)
    pair = start >> 1
    info[...] = jnp.full((1, BLOCK), pair, jnp.int32)
    recv_info[gy] = jnp.full((1, BLOCK), pair, jnp.int32)

    def group_of(first, j, t):
        begin = (first - j + 15) >> 4
        return (t + 4 * ((begin - t + 3) >> 2)) & (COLS - 1)

    row = lax.broadcasted_iota(jnp.int32, (8, BLOCK), 0)
    lane = lax.broadcasted_iota(jnp.int32, (8, BLOCK), 1)
    occ_parts = [
        jnp.broadcast_to(occ[:, c : c + BLOCK], (8, BLOCK)).astype(jnp.float32)
        for c in range(0, NBLK, BLOCK)
    ]

    @pl.loop(0, ROWS, unroll=4)
    def _(j):
        block = group_of(pair, j, row >> 1) * GROUP + 2 * j + (row & 1)
        mine = jnp.zeros((8, BLOCK), jnp.float32)
        for c, part in enumerate(occ_parts):
            mine = mine + jnp.where(lane == block - c * BLOCK, part, 0.0)
        mine = jnp.sum(mine, axis=1, keepdims=True)
        occ_rows[j] = jnp.broadcast_to(mine, (8, BLOCK))

    pl.semaphore_wait(
        barrier, jnp.where(gx == HUB, 0, 1) + jnp.where(gy < HALF, HALF - 1, HALF)
    )

    @pl.when(gx != HUB)
    def _():
        pl.semaphore_signal(row_sem, inc=1, device_id={"gx": HUB}, device_id_type=MESH)

    @pl.when(gy >= HALF)
    def _():
        @pl.loop(0, HALF)
        def _(j):
            pl.semaphore_signal(late_sem, inc=1, device_id={"gy": j}, device_id_type=MESH)

    for copy in large:
        copy.wait()

    def shade(j):
        for t in range(4):
            group = group_of(pair, j, t)
            for h in range(2):
                k = 2 * t + h
                block = group * GROUP + 2 * j + h
                to = pl.ds(pl.multiple_of(j * 64 + k * 8, 8), 8)
                dens_rows[to, :] = dens[block].astype(jnp.float32)
                src_rows[to, :] = src[block].astype(jnp.float32)
        occupied = occ_rows[j]
        color = jnp.zeros((8, BLOCK), jnp.float32)
        trans = jnp.ones((8, BLOCK), jnp.float32)
        for s in range(DEPTH):
            cut = pl.ds(j * 64 + s, 8, stride=8)
            fade = jnp.exp(-(dens_rows[cut, :] * occupied))
            color = color + trans * src_rows[cut, :] * (1.0 - fade)
            trans = trans * fade
        return color, trans

    def send(j):
        @pl.when(j != gy)
        def _():
            for part, (ours, theirs) in enumerate(((send1.at[j], recv1), (info, recv_info))):
                pltpu.make_async_remote_copy(
                    src_ref=ours,
                    dst_ref=theirs.at[gy],
                    send_sem=send_sems.at[part],
                    recv_sem=recv_sems.at[part],
                    device_id={"gy": j},
                    device_id_type=MESH,
                ).start()

    def peer(d, half):
        return half * HALF + (lax.rem(gy, HALF) ^ (HALF - 1 - d))

    @pl.loop(0, HALF)
    def _(d):
        j = peer(d, 0)
        color, trans = shade(j)
        send1[j, 0] = color
        send1[j, 1] = trans
        send(j)

    @pl.loop(0, HALF)
    def _(d):
        j = peer(d, 1)
        color, trans = shade(j)
        send1[j, 0] = color
        send1[j, 1] = trans

    @pl.when(gy < HALF)
    def _():
        pl.semaphore_wait(late_sem, HALF)
        pl.semaphore_signal(go_sem, inc=1, device_id={"gy": gy + HALF}, device_id_type=MESH)

    @pl.when(gy >= HALF)
    def _():
        pl.semaphore_wait(go_sem, 1)

    @pl.loop(0, HALF)
    def _(d):
        send(peer(d, 1))

    recv1[gy] = send1[gy]

    @pl.when(gx == HUB)
    def _():
        pl.semaphore_wait(row_sem, COLS - 1)

        @pl.loop(1, COLS)
        def _(i):
            pl.semaphore_signal(row_go_sem, inc=1, device_id={"gx": lax.rem(HUB + i, COLS)}, device_id_type=MESH)

    for part, ref in enumerate((recv1, recv_info)):
        others = ref.at[pl.ds(0, ROWS - 1)]
        pltpu.make_async_copy(others, others, recv_sems.at[part]).wait()
    small[1].wait()
    small[2].wait()

    t_of = lax.broadcasted_iota(jnp.int32, (8, BLOCK), 0) >> 1

    def over_row(k, carry):
        total, remain = carry
        r = row_ref[k]
        color = recv1[r, 0]
        trans = recv1[r, 1]
        first = jnp.broadcast_to(recv_info[r], (8, BLOCK))
        place = group_of(first, gy, t_of) >> 2
        new_total, new_remain = [], []
        for v in range(8):
            here = place == v
            new_total.append(total[v] + remain[v] * jnp.where(here, color, 0.0))
            new_remain.append(remain[v] * jnp.where(here, trans, 1.0))
        return tuple(new_total), tuple(new_remain)

    zeros = tuple(jnp.zeros((8, BLOCK), jnp.float32) for _ in range(8))
    ones = tuple(jnp.ones((8, BLOCK), jnp.float32) for _ in range(8))
    total, remain = lax.fori_loop(0, ROWS, over_row, (zeros, ones), unroll=4)
    for v in range(8):
        for t in range(4):
            send2[4 * v + t, 0] = total[v][2 * t : 2 * t + 2]
            send2[4 * v + t, 1] = remain[v][2 * t : 2 * t + 2]

    @pl.when(gx != HUB)
    def _():
        pl.semaphore_wait(row_go_sem, 1)

    @pl.loop(0, COLS - 1)
    def _(d):
        i = column_peer(gx, d)
        pltpu.make_async_remote_copy(
            src_ref=send2.at[i],
            dst_ref=recv2.at[gx],
            send_sem=send_sems.at[2],
            recv_sem=recv_sems.at[2],
            device_id={"gx": i},
            device_id_type=MESH,
        ).start()

    recv2[gx] = send2[gx]
    others2 = recv2.at[pl.ds(0, COLS - 1)]
    pltpu.make_async_copy(others2, others2, recv_sems.at[2]).wait()

    def over_column(k, carry):
        total, remain = carry
        c = col_ref[k]
        return total + remain * recv2[c, 0], remain * recv2[c, 1]

    total, remain = lax.fori_loop(
        0,
        COLS,
        over_column,
        (jnp.zeros((2, BLOCK), jnp.float32), jnp.ones((2, BLOCK), jnp.float32)),
        unroll=8,
    )
    out_ref[0] = total
    out_ref[1] = remain

    for part, ref in enumerate((recv1, recv_info)):
        others = ref.at[pl.ds(0, ROWS - 1)]
        pltpu.make_async_copy(others, others, send_sems.at[part]).wait()
    pltpu.make_async_copy(others2, others2, send_sems.at[2]).wait()


def deliver(both_ref, emission_ref, transmittance_ref):
    emission_ref[...] = both_ref[0]
    transmittance_ref[...] = both_ref[1]


def on_device(density, source, occupancy, row_order, col_order):
    vmem = pl.BlockSpec(memory_space=pltpu.VMEM)
    hbm = pl.BlockSpec(memory_space=pltpu.HBM)
    density, source = (
        a.reshape(DEPTH, NBLK, BLOCK).transpose(1, 0, 2) for a in (density, source)
    )
    operands = [
        pltpu.with_memory_space_constraint(a, pltpu.HBM)
        for a in (density, source, occupancy, row_order, col_order)
    ]
    both = pl.pallas_call(
        kernel,
        out_shape=pltpu.VMEM((2, 2, BLOCK), jnp.float32),
        in_specs=[hbm] * 5,
        out_specs=vmem,
        scratch_shapes=[
            pltpu.VMEM((1, 1, NBLK), jnp.int32),
            pltpu.SMEM((ROWS,), jnp.int32),
            pltpu.SMEM((COLS,), jnp.int32),
            pltpu.VMEM((NBLK, DEPTH, BLOCK), jnp.bfloat16),
            pltpu.VMEM((NBLK, DEPTH, BLOCK), jnp.bfloat16),
            pltpu.VMEM((ROWS * 64, BLOCK), jnp.float32),
            pltpu.VMEM((ROWS * 64, BLOCK), jnp.float32),
            pltpu.VMEM((ROWS, 8, BLOCK), jnp.float32),
            pltpu.VMEM((ROWS, 2, 8, BLOCK), jnp.float32),
            pltpu.VMEM((ROWS, 2, 8, BLOCK), jnp.float32),
            pltpu.VMEM((1, BLOCK), jnp.int32),
            pltpu.VMEM((ROWS, 1, BLOCK), jnp.int32),
            pltpu.VMEM((COLS, 2, 2, BLOCK), jnp.float32),
            pltpu.VMEM((COLS, 2, 2, BLOCK), jnp.float32),
            pltpu.SemaphoreType.DMA((5,)),
            pltpu.SemaphoreType.DMA((3,)),
            pltpu.SemaphoreType.DMA((3,)),
            pltpu.SemaphoreType.REGULAR,
            pltpu.SemaphoreType.REGULAR,
            pltpu.SemaphoreType.REGULAR,
            pltpu.SemaphoreType.REGULAR,
        ],
        compiler_params=pltpu.CompilerParams(
            collective_id=0, has_side_effects=True, vmem_limit_bytes=40 * 1024 * 1024
        ),
    )(*operands)
    out = jax.ShapeDtypeStruct((2, BLOCK), jnp.float32)
    emission, transmittance = pl.pallas_call(
        deliver,
        out_shape=(out, out),
        in_specs=[vmem],
        out_specs=(vmem, vmem),
        compiler_params=pltpu.CompilerParams(vmem_limit_bytes=2**20),
    )(both)
    return emission.reshape(2 * BLOCK), transmittance.reshape(2 * BLOCK)


def solution(mesh):
    placed = (P("gx", "gy", None, None), P("gx", "gy", None, None), P("gx", "gy", None), P(), P())
    return jax.shard_map(
        on_device,
        mesh=mesh,
        in_specs=placed,
        out_specs=(P(("gx", "gy")), P(("gx", "gy"))),
        check_vma=False,
    )
```
